1024 devices in a mesh: row: 16 (over z_hi, x), col: 64 (over z_lo, y, core).
Axes of the slice: x: 8, y: 8, z: 8 (z_hi: 2, z_lo: 4; z = z_hi * 4 + z_lo), core: 2. Of those that a mesh axis runs over, the one named last changes fastest.
Arguments:
- integrals: float32 [9600, 76800], P('row', 'col'), may hold values from -0.0234375 to 0.0234375
- amplitudes: float32 [512, 64, 1200], P('col', None, 'row'), may hold values from -16 to 16
- old_amps: float32 [512, 9600], P('col', 'row'), may hold values from -2 to 2
- other_terms: float32 [512, 9600], P('col', 'row'), may hold values from -6 to 6
- occ_energy: float32 [128], replicated, may hold values from -2 to -0.5
- vir_energy: float32 [1200], replicated, may hold values from 0.2 to 4
- pair_occ: int32 [512, 2], P('col'), may hold values from 0 to 127
- a_orbitals: int32 [8], replicated, may hold values from 0 to 1199
Outputs:
- new_amps: float32 [512, 9600], P('col', 'row')
The draws below stay inside these ranges and needn't reach their ends.
All inputs are finite; a program needn't handle non-finite values.
Results may differ from the reference program's by a relative error of at most 0.00005.
Values sent between devices are 32-bit elements; how exact they have to be, the bound alone decides.
A program may use at most 32 MiB of HBM per device.

```python
import math
import jax
import jax.numpy as jnp
from jax import lax

NV = 1200
NOCC = 128
PAIRS = 512
A_WIN = 8
C_WIN = 64
AB = 9600
CD = 76800


def place_ends(array, key, low, high):
    longest = array.shape.index(max(array.shape))
    spots = []
    for shift in (0, 1):
        where = [jax.random.randint(jax.random.fold_in(key, axis), (), 0, length) for axis, length in enumerate(array.shape)]
        where[longest] = (where[longest] + shift) % array.shape[longest]
        spots.append(tuple(where))
    return array.at[spots[0]].set(low).at[spots[1]].set(high)


def raised(drawn, own_key, source, target, shards_of, factor):
    def block_of(axis_at):
        return (jnp.arange(drawn.shape[axis_at]) // (drawn.shape[axis_at] // shards_of)).reshape((-1,) + (1,) * (drawn.ndim - 1 - axis_at))

    near = jax.random.permutation(own_key, shards_of)[block_of(target)]
    far = (block_of(target) + shards_of // 2) % shards_of
    return jnp.where((block_of(source) == near) | (block_of(source) == far), factor * drawn, drawn)


def steps_of(rng, dims, cuts, least, high):
    def one(axis_at, parts):
        steps = jax.random.uniform(jax.random.fold_in(jax.random.fold_in(rng, 6), axis_at), (parts,), jnp.float32, least / len(cuts), high / len(cuts))
        return jnp.repeat(jnp.exp(steps), dims[axis_at] // parts).reshape((-1,) + (1,) * (len(dims) - axis_at - 1))

    level = one(*cuts[0])
    for cut in cuts[1:]:
        level = level * one(*cut)
    return level


def scatter_about(rng, dims, spread, reach, pieces=(), held_as=jnp.bfloat16):
    level = steps_of(rng, dims, pieces, -0.22, 0.18) if pieces else 1.0
    entries = jax.random.normal(rng, dims, jnp.float32) * spread * level
    return jnp.minimum(jnp.maximum(entries, -reach), reach).astype(held_as)


def gaussian_with(key, extent, scale, bound, pieces, heavy, dtype=jnp.bfloat16):
    entries = scale * jax.random.normal(key, extent, jnp.float32)
    if pieces:
        entries = entries * steps_of(key, extent, pieces, -0.22, 0.18)
    return jnp.clip(raised(entries, jax.random.fold_in(key, 3), *heavy), -bound, bound).astype(dtype)


def setup_inputs(seed: int = 0) -> dict:
    splits = jax.random.split(jax.random.key(seed), 9)
    integrals = scatter_about(splits[0], (AB, CD), CD ** -0.5, 0.0234375, ((0, 16), (1, 64)), jnp.float32)
    amplitudes = gaussian_with(splits[1], (PAIRS, C_WIN, NV), 1.0, 16.0, ((0, 64), (2, 16)), (1, 0, 64, 4.0), jnp.float32)
    old_amps = scatter_about(splits[2], (PAIRS, AB), 0.3, 2.0, ((0, 64), (1, 16)), jnp.float32)
    other_terms = scatter_about(splits[3], (PAIRS, AB), 1.0, 6.0, ((0, 64), (1, 16)), jnp.float32)
    occ_energy = jnp.clip(jax.random.uniform(splits[4], (NOCC,), jnp.float32, -2.0, -0.5), -2.0, -0.5)
    vir_energy = jnp.clip(jnp.exp(jax.random.uniform(splits[5], (NV,), jnp.float32, math.log(0.2), math.log(4.0))), 0.2, 4.0)
    pair_occ = place_ends(jax.random.randint(splits[6], (PAIRS, 2), 0, NOCC), jax.random.fold_in(splits[6], 1), 0, NOCC - 1).astype(jnp.int32)
    a_orbitals = place_ends(jax.random.randint(splits[7], (A_WIN,), 0, NV), jax.random.fold_in(splits[7], 1), 0, NV - 1).astype(jnp.int32)
    return dict(integrals=integrals, amplitudes=amplitudes, old_amps=old_amps, other_terms=other_terms, occ_energy=occ_energy, vir_energy=vir_energy, pair_occ=pair_occ, a_orbitals=a_orbitals)


def reference(integrals, amplitudes, old_amps, other_terms, occ_energy, vir_energy, pair_occ, a_orbitals):
    flat_amps = amplitudes.reshape(PAIRS, C_WIN * NV)
    ladder = jnp.dot(flat_amps, integrals.T, precision=lax.Precision.HIGHEST, preferred_element_type=jnp.float32)
    occ_pair = occ_energy[pair_occ[:, 0]] + occ_energy[pair_occ[:, 1]]
    vir_pair = (vir_energy[a_orbitals][:, None] + vir_energy[None, :]).reshape(A_WIN * NV)
    denom = occ_pair[:, None] - vir_pair[None, :]
    return old_amps + (ladder + other_terms) / denom
```

```python
import jax
import jax.numpy as jnp
from jax import lax
from jax.experimental import pallas as pl
from jax.experimental.pallas import tpu as pltpu
from jax.sharding import PartitionSpec as P

NV = 1200
MESH = pl.DeviceIdType.MESH
X = 8
PLANE = 16
STAGES = 4
ROWS = 16
DEPTH = 75
UNIT = 80
AB = 600
ABP = 640
F32 = jnp.float32
BF16 = jnp.bfloat16

RIGHT_OWN, RIGHT_OTHER, LEFT_OWN, LEFT_OTHER = 0, 4, 7, 10


def kernel(
    integrals_ref,
    amps_ref,
    old_ref,
    other_ref,
    occ_ref,
    vir_ref,
    pair_ref,
    aorb_ref,
    out_ref,
    integ,
    staged,
    relay,
    tiles,
    units,
    factors,
    total,
    partial,
    from_core,
    from_y,
    to_z,
    from_z,
    integ_sem,
    bundle_send,
    bundle_recv,
    tile_send,
    tile_recv,
    unit_send,
    unit_recv,
    core_send,
    core_recv,
    y_send,
    y_recv,
    z_send,
    z_recv,
):
    r = lax.axis_index("row")
    k = lax.axis_index("col")
    x, zh = r % X, r // X
    zl, m = k // PLANE, k % PLANE
    y, core = m // 2, m % 2
    right = zh * X + (x + 1) % X
    left = zh * X + (x + X - 1) % X
    facing = (r + X) % ROWS

    load = pltpu.make_async_copy(integrals_ref, integ, integ_sem)
    load.start()

    barrier = pltpu.get_barrier_semaphore()

    def greet(row, col):
        pl.semaphore_signal(barrier, inc=1, device_id=(row, col), device_id_type=MESH)

    def greet_plane(j, carry):
        greet(r, zl * PLANE + (m + j) % PLANE)
        return carry

    lax.fori_loop(1, PLANE, greet_plane, 0)
    for j in range(1, STAGES):
        greet(r, ((zl + j) % STAGES) * PLANE + m)
    greet(right, k)
    greet(left, k)
    greet(facing, k)

    def stage_tiles(o, carry):
        for j in range(8):
            c = o * 8 + j
            staged[c] = jnp.zeros((8, 128), F32)
            staged[c, :, 0:DEPTH] = amps_ref[pl.ds(c, 8, stride=64), :]
        return carry

    lax.fori_loop(0, 8, stage_tiles, 0)
    pl.semaphore_wait(barrier, PLANE - 1 + STAGES - 1 + 3)

    def send_tiles(i, source, base):
        def one(j, carry):
            t = (m + j) % PLANE
            pltpu.make_async_remote_copy(
                src_ref=source.at[base + t],
                dst_ref=tiles.at[i, m],
                send_sem=tile_send.at[i],
                recv_sem=tile_recv.at[i],
                device_id=(r, zl * PLANE + t),
                device_id_type=MESH,
            ).start()
            return carry

        lax.fori_loop(1, PLANE, one, 0)
        tiles[i, m] = source[base + m]

    def bundle(i):
        plane = (zl + STAGES - i) % STAGES
        return pltpu.make_async_remote_copy(
            src_ref=staged.at[pl.ds(plane * PLANE, PLANE)],
            dst_ref=relay.at[pl.ds(i * PLANE, PLANE)],
            send_sem=bundle_send.at[i],
            recv_sem=bundle_recv.at[i],
            device_id=(r, plane * PLANE + m),
            device_id_type=MESH,
        )

    send_tiles(0, staged, zl * PLANE)
    for i in range(1, STAGES):
        bundle(i).start()

    load.wait()

    def make_factors(d, rows, count):
        lane = lax.broadcasted_iota(jnp.int32, (count, 128), 1)
        first, off = (DEPTH * d) // 128 * 128, (DEPTH * d) % 128

        def tile_at(start):
            width = min(128, NV - start)
            v = integ[rows, start : start + width]
            if width < 128:
                v = jnp.concatenate([v, jnp.zeros((count, 128 - width), F32)], axis=1)
            return v

        v = tile_at(first)
        if off:
            v = pltpu.roll(v, 128 - off, 1)
        if off + DEPTH > 128:
            v = jnp.where(lane < 128 - off, v, pltpu.roll(tile_at(first + 128), 128 - off, 1))
        v = jnp.where(lane < DEPTH, v, 0.0)
        hi = v.astype(BF16).astype(F32)
        lo = pltpu.roll(v - hi, UNIT, 1)
        return (
            (hi + jnp.where(lane >= UNIT, lo, 0.0)).astype(BF16),
            (pltpu.roll(hi, 2 * UNIT - 128, 1) + jnp.where(lane < 32, lo, 0.0)).astype(BF16),
        )

    for d in range(ROWS):

        def chunk(n, carry, d=d):
            rows = pl.ds(pl.multiple_of(n * 128, 128), 128)
            a, b = make_factors(d, rows, 128)
            factors[d, rows, 0:128] = a
            factors[d, rows, 128:256] = b
            return carry

        lax.fori_loop(0, 4, chunk, 0)
        a, b = make_factors(d, slice(512, AB), AB - 512)
        pad = jnp.zeros((ABP - AB, 128), BF16)
        factors[d, 512:ABP, 0:128] = jnp.concatenate([a, pad], axis=0)
        factors[d, 512:ABP, 128:256] = jnp.concatenate([b, pad], axis=0)

    def hop(i, lane, h):
        to_right = lane in (RIGHT_OWN, RIGHT_OTHER)
        own = lane in (RIGHT_OWN, LEFT_OWN)
        at = (x + X - (h - 1)) % X if to_right else (x + h - 1) % X
        origin = (zh if own else 1 - zh) * X + at
        return pltpu.make_async_remote_copy(
            src_ref=units.at[i, origin],
            dst_ref=units.at[i, origin],
            send_sem=unit_send.at[i],
            recv_sem=unit_recv.at[i, lane + h],
            device_id=(right if to_right else left, k),
            device_id_type=MESH,
        )

    def land(i, lane, h):
        to_right = lane in (RIGHT_OWN, RIGHT_OTHER)
        own = lane in (RIGHT_OWN, LEFT_OWN)
        at = (x + X - h) % X if to_right else (x + h) % X
        origin = (zh if own else 1 - zh) * X + at
        pltpu.make_async_remote_copy(
            src_ref=units.at[i, origin],
            dst_ref=units.at[i, origin],
            send_sem=unit_send.at[i],
            recv_sem=unit_recv.at[i, lane + h],
            device_id=(right, k),
            device_id_type=MESH,
        ).wait_recv()
        return origin

    def across(i, origin):
        return pltpu.make_async_remote_copy(
            src_ref=units.at[i, origin],
            dst_ref=units.at[i, origin],
            send_sem=unit_send.at[i],
            recv_sem=unit_recv.at[i, 0],
            device_id=(facing, k),
            device_id_type=MESH,
        )

    def add(i, origin, first=False):
        a = units[i, origin]
        hi = a.astype(BF16)
        lo = (a - hi.astype(F32)).astype(BF16)
        rhs = jnp.concatenate([hi, hi, lo, jnp.zeros((256 - 3 * UNIT, 128), BF16)], axis=0)
        product = jnp.dot(factors[origin], rhs, preferred_element_type=F32)
        if first:
            total[i] = product
        else:
            total[i] += product

    def begin(i):
        pltpu.make_async_copy(
            tiles.at[i, pl.ds(0, PLANE - 1)], tiles.at[i, pl.ds(0, PLANE - 1)], tile_recv.at[i]
        ).wait()
        units[i, r] = jnp.transpose(tiles[i].reshape(128, 128))[0:UNIT]
        across(i, r).start()
        hop(i, RIGHT_OWN, 1).start()
        hop(i, LEFT_OWN, 1).start()

    def pass_on(i):
        bundle(i).wait_recv()
        send_tiles(i, relay, i * PLANE)

    def step(i, s):
        got = []
        if s == 1:
            across(i, facing).wait_recv()
            hop(i, RIGHT_OTHER, 1).start()
            hop(i, LEFT_OTHER, 1).start()
            got.append(facing)
        for lane, hops, h in (
            (RIGHT_OWN, 4, s),
            (LEFT_OWN, 3, s),
            (RIGHT_OTHER, 3, s - 1),
            (LEFT_OTHER, 4, s - 1),
        ):
            if 1 <= h <= hops:
                got.append(land(i, lane, h))
                if h < hops:
                    hop(i, lane, h + 1).start()
        return got

    def core_copy(i):
        return pltpu.make_async_remote_copy(
            src_ref=partial.at[i, 1 - core],
            dst_ref=from_core.at[i],
            send_sem=core_send.at[i],
            recv_sem=core_recv.at[i],
            device_id=(r, zl * PLANE + y * 2 + 1 - core),
            device_id_type=MESH,
        )

    def sum_cores(i):
        ladder = jnp.transpose(total[i])
        for t in range(PLANE):
            partial[i, t % 2, t // 2] = ladder[8 * t : 8 * t + 8]
        core_copy(i).start()

    def sum_y(i):
        core_copy(i).wait_recv()
        partial[i, core] = partial[i, core] + from_core[i]

        def one(j, carry):
            t = (y + j) % 8
            pltpu.make_async_remote_copy(
                src_ref=partial.at[i, core, t],
                dst_ref=from_y.at[i, y],
                send_sem=y_send.at[i],
                recv_sem=y_recv.at[i],
                device_id=(r, zl * PLANE + t * 2 + core),
                device_id_type=MESH,
            ).start()
            return carry

        lax.fori_loop(1, 8, one, 0)
        from_y[i, y] = partial[i, core, y]

    def z_copy(i):
        return pltpu.make_async_remote_copy(
            src_ref=to_z.at[i],
            dst_ref=from_z.at[i],
            send_sem=z_send.at[i],
            recv_sem=z_recv.at[i],
            device_id=(r, ((zl + i) % STAGES) * PLANE + m),
            device_id_type=MESH,
        )

    def sum_z(i):
        seven = from_y.at[i, pl.ds(0, 7)]
        pltpu.make_async_copy(seven, seven, y_recv.at[i]).wait()
        value = from_y[i, 0]
        for j in range(1, 8):
            value = value + from_y[i, j]
        to_z[i] = value

    def drain(i):
        some = units.at[i, pl.ds(0, 15)]
        pltpu.make_async_copy(some, some, unit_send.at[i]).wait()
        some = tiles.at[i, pl.ds(0, PLANE - 1)]
        pltpu.make_async_copy(some, some, tile_send.at[i]).wait()
        core_copy(i).wait_send()
        some = from_y.at[i, pl.ds(0, 7)]
        pltpu.make_async_copy(some, some, y_send.at[i]).wait()

    def turn(n, carry):
        @pl.when(n < STAGES)
        def _():
            begin(n)

        @pl.when((n >= 1) & (n < STAGES + 1))
        def _():
            origins = step(n - 1, 2)
            for origin in origins:
                add(n - 1, origin)

        @pl.when(n >= 2)
        def _():
            origins = step(n - 2, 4)
            for origin in origins:
                add(n - 2, origin)

        @pl.when(n < STAGES)
        def _():
            add(n, r, first=True)

        @pl.when(n < STAGES - 1)
        def _():
            pass_on(n + 1)

        @pl.when(n >= 3)
        def _():
            sum_y(n - 3)

        @pl.when(n < STAGES)
        def _():
            origins = step(n, 1)
            for origin in origins:
                add(n, origin)

        @pl.when((n >= 1) & (n < STAGES + 1))
        def _():
            origins = step(n - 1, 3)
            for origin in origins:
                add(n - 1, origin)

        @pl.when(n >= 2)
        def _():
            origins = step(n - 2, 5)
            for origin in origins:
                add(n - 2, origin)
            sum_cores(n - 2)

        @pl.when(n >= 3)
        def _():
            sum_z(n - 3)

        @pl.when(n >= 4)
        def _():
            z_copy(n - 3).start()

        @pl.when(n >= 3)
        def _():
            drain(n - 3)

        return carry

    lax.fori_loop(0, STAGES + 2, turn, 0)

    last = STAGES - 1
    sum_y(last)

    pair = pair_ref[...]
    table = lax.broadcasted_iota(jnp.int32, (8, 128), 1)
    occ = occ_ref[...]
    occ_first = jnp.sum(jnp.where(pair[:, 0:1] == table, occ, 0.0), axis=1, keepdims=True)
    occ_second = jnp.sum(jnp.where(pair[:, 1:2] == table, occ, 0.0), axis=1, keepdims=True)
    vir = vir_ref[...]
    blocks = lax.broadcasted_iota(jnp.int32, (1, 8), 1)
    a_pick = jnp.sum(
        jnp.where(blocks == r // 2, aorb_ref[...].astype(F32), 0.0), axis=1, keepdims=True
    )
    orbitals = lax.broadcasted_iota(jnp.int32, (1, NV), 1).astype(F32)
    vir_a = jnp.sum(jnp.where(orbitals == a_pick, vir, 0.0), axis=1, keepdims=True)
    vir_b = jnp.where(r % 2 == 0, vir[:, 0:AB], vir[:, AB:NV])
    denom = (occ_first + occ_second) - (vir_a + vir_b)

    sum_z(last)
    z_copy(last).start()
    for i in range(1, STAGES):
        bundle(i).wait_send()
    drain(last)
    ladder = to_z[0]
    for i in range(1, STAGES):
        z_copy(i).wait_recv()
        ladder = ladder + from_z[i]
    out_ref[...] = old_ref[...] + (ladder[:, 0:AB] + other_ref[...]) / denom
    for i in range(1, STAGES):
        z_copy(i).wait_send()


def local(
    integrals, amplitudes, old_amps, other_terms, occ_energy, vir_energy, pair_occ, a_orbitals
):
    vmem = pl.BlockSpec(memory_space=pltpu.VMEM)
    dma = pltpu.SemaphoreType.DMA
    return pl.pallas_call(
        kernel,
        out_shape=jax.ShapeDtypeStruct((8, AB), F32),
        in_specs=[pl.BlockSpec(memory_space=pl.ANY)] + [vmem] * 7,
        out_specs=vmem,
        scratch_shapes=[
            pltpu.VMEM((AB, NV), F32),
            pltpu.VMEM((64, 8, 128), F32),
            pltpu.VMEM((64, 8, 128), F32),
            pltpu.VMEM((STAGES, PLANE, 8, 128), F32),
            pltpu.VMEM((STAGES, ROWS, UNIT, 128), F32),
            pltpu.VMEM((ROWS, ABP, 256), BF16),
            pltpu.VMEM((STAGES, ABP, 128), F32),
            pltpu.VMEM((STAGES, 2, 8, 8, ABP), F32),
            pltpu.VMEM((STAGES, 8, 8, ABP), F32),
            pltpu.VMEM((STAGES, 8, 8, ABP), F32),
            pltpu.VMEM((STAGES, 8, ABP), F32),
            pltpu.VMEM((STAGES, 8, ABP), F32),
            dma,
            dma((STAGES,)),
            dma((STAGES,)),
            dma((STAGES,)),
            dma((STAGES,)),
            dma((STAGES,)),
            dma((STAGES, 15)),
            dma((STAGES,)),
            dma((STAGES,)),
            dma((STAGES,)),
            dma((STAGES,)),
            dma((STAGES,)),
            dma((STAGES,)),
        ],
        compiler_params=pltpu.CompilerParams(
            collective_id=0, has_side_effects=True, vmem_limit_bytes=40 * 1024 * 1024
        ),
        cost_estimate=pl.CostEstimate(
            flops=6 * 512 * AB * NV, bytes_accessed=4 * AB * NV, transcendentals=0
        ),
    )(
        integrals,
        amplitudes.reshape(8 * 64, DEPTH),
        old_amps,
        other_terms,
        occ_energy.reshape(1, -1),
        vir_energy.reshape(1, -1),
        pair_occ,
        a_orbitals.reshape(1, -1),
    )


def solution(mesh):
    in_specs = (
        P("row", "col"),
        P("col", None, "row"),
        P("col", "row"),
        P("col", "row"),
        P(),
        P(),
        P("col", None),
        P(),
    )
    out_specs = P("col", "row")
    return jax.shard_map(local, mesh=mesh, in_specs=in_specs, out_specs=out_specs, check_vma=False)
```

```python
import jax
import jax.numpy as jnp
from jax import lax
from jax.experimental import pallas as pl
from jax.experimental.pallas import tpu as pltpu
from jax.sharding import PartitionSpec as P

NV = 1200
MESH = pl.DeviceIdType.MESH
X = 8
PLANE = 16
STAGES = 4
ROWS = 16
DEPTH = 75
UNIT = 80
AB = 600
ABP = 640
NVP = 1280
WINDOW = 768
SHIFT = 88
F32 = jnp.float32
BF16 = jnp.bfloat16

RIGHT_OWN, RIGHT_OTHER, LEFT_OWN, LEFT_OTHER = 0, 4, 7, 10


def far_first(n, count):
    return count // 2 + (n + 1) // 2 * (1 - 2 * (n % 2))


def kernel(
    integrals_hbm,
    amps_hbm,
    old_hbm,
    other_hbm,
    occ_hbm,
    vir_hbm,
    pair_hbm,
    aorb_hbm,
    out_ref,
    integ,
    amps_ref,
    old_ref,
    other_ref,
    occ_ref,
    vir_ref,
    pair_ref,
    aorb_ref,
    staged,
    relay,
    tiles,
    units,
    high,
    low,
    panel,
    total,
    partial,
    from_core,
    from_y,
    to_z,
    from_z,
    facing_here,
    load_sem,
    bundle_send,
    bundle_recv,
    tile_send,
    tile_recv,
    unit_send,
    unit_recv,
    core_send,
    core_recv,
    y_send,
    y_recv,
    z_send,
    z_recv,
):
    r = lax.axis_index("row")
    k = lax.axis_index("col")
    x, zh = r % X, r // X
    zl, m = k // PLANE, k % PLANE
    y, core = m // 2, m % 2
    right = zh * X + (x + 1) % X
    left = zh * X + (x + X - 1) % X
    facing = (r + X) % ROWS

    loads = [
        pltpu.make_async_copy(source, target, load_sem.at[n])
        for n, (source, target) in enumerate(
            (
                (amps_hbm, amps_ref),
                (integrals_hbm, integ),
                (old_hbm, old_ref),
                (other_hbm, other_ref),
                (occ_hbm, occ_ref),
                (vir_hbm, vir_ref),
                (pair_hbm, pair_ref),
                (aorb_hbm, aorb_ref),
            )
        )
    ]
    loads[0].start()

    barrier = pltpu.get_barrier_semaphore()

    def greet(row, col):
        pl.semaphore_signal(barrier, inc=1, device_id=(row, col), device_id_type=MESH)

    def greet_plane(j, carry):
        greet(r, zl * PLANE + (m + j) % PLANE)
        return carry

    lax.fori_loop(1, PLANE, greet_plane, 0)
    for j in range(1, STAGES):
        greet(r, ((zl + j) % STAGES) * PLANE + m)
    greet(right, k)
    greet(left, k)

    @pl.when(zh == 0)
    def _():
        greet(facing, k)


    def stage_tiles(o, carry):
        for j in range(8):
            c = o * 8 + j
            staged[c] = jnp.zeros((8, 128), F32)
            staged[c, :, 0:DEPTH] = amps_ref[pl.ds(c, 8, stride=64), :]
        return carry

    loads[0].wait()
    for load in loads[1:]:
        load.start()
    lax.fori_loop(0, 8, stage_tiles, 0)
    pl.semaphore_wait(barrier, PLANE - 1 + STAGES - 1 + 2 + zh)

    @pl.when(zh == 1)
    def _():
        pl.semaphore_signal(facing_here, inc=1, device_id=(facing, k), device_id_type=MESH)


    def send_tiles(i, source, base):
        def one(n, carry):
            t = (m + far_first(n, PLANE)) % PLANE
            pltpu.make_async_remote_copy(
                src_ref=source.at[base + t],
                dst_ref=tiles.at[i, m],
                send_sem=tile_send.at[i],
                recv_sem=tile_recv.at[i],
                device_id=(r, zl * PLANE + t),
                device_id_type=MESH,
            ).start()
            return carry

        lax.fori_loop(0, PLANE - 1, one, 0)
        tiles[i, m] = source[base + m]

    def bundle(i):
        plane = (zl + STAGES - i) % STAGES
        return pltpu.make_async_remote_copy(
            src_ref=staged.at[pl.ds(plane * PLANE, PLANE)],
            dst_ref=relay.at[pl.ds(i * PLANE, PLANE)],
            send_sem=bundle_send.at[i],
            recv_sem=bundle_recv.at[i],
            device_id=(r, plane * PLANE + m),
            device_id_type=MESH,
        )

    send_tiles(0, staged, zl * PLANE)
    for i in range(1, STAGES):
        bundle(i).start()

    def split(v):
        hi = v.astype(BF16)
        return hi, (v - hi.astype(F32)).astype(BF16)

    def split_integrals():
        loads[1].wait()
        last = NV // 128 * 128
        for part in (high, low):
            part[:, last:] = jnp.zeros((ABP, NVP - last), BF16)

        def chunk(n, carry):
            rows = pl.ds(pl.multiple_of(n * 128, 128), 128)
            hi, lo = split(integ[rows, :])
            high[rows, 0:NV] = hi
            low[rows, 0:NV] = lo
            return carry

        lax.fori_loop(0, 4, chunk, 0)
        pad = jnp.zeros((ABP - AB, NV), BF16)
        hi, lo = split(integ[512:AB, :])
        high[512:ABP, 0:NV] = jnp.concatenate([hi, pad], axis=0)
        low[512:ABP, 0:NV] = jnp.concatenate([lo, pad], axis=0)

    def hop(i, lane, h):
        to_right = lane in (RIGHT_OWN, RIGHT_OTHER)
        own = lane in (RIGHT_OWN, LEFT_OWN)
        at = (x + X - (h - 1)) % X if to_right else (x + h - 1) % X
        origin = (zh if own else 1 - zh) * X + at
        return pltpu.make_async_remote_copy(
            src_ref=units.at[i, origin],
            dst_ref=units.at[i, origin],
            send_sem=unit_send.at[i],
            recv_sem=unit_recv.at[i, lane + h],
            device_id=(right if to_right else left, k),
            device_id_type=MESH,
        )

    def land(i, lane, h):
        to_right = lane in (RIGHT_OWN, RIGHT_OTHER)
        own = lane in (RIGHT_OWN, LEFT_OWN)
        at = (x + X - h) % X if to_right else (x + h) % X
        origin = (zh if own else 1 - zh) * X + at
        pltpu.make_async_remote_copy(
            src_ref=units.at[i, origin],
            dst_ref=units.at[i, origin],
            send_sem=unit_send.at[i],
            recv_sem=unit_recv.at[i, lane + h],
            device_id=(right, k),
            device_id_type=MESH,
        ).wait_recv()
        return origin

    def across(i, origin):
        return pltpu.make_async_remote_copy(
            src_ref=units.at[i, origin],
            dst_ref=units.at[i, origin],
            send_sem=unit_send.at[i],
            recv_sem=unit_recv.at[i, 0],
            device_id=(facing, k),
            device_id_type=MESH,
        )

    def add(i, plane):
        for u in range(X):
            panel[plane, pl.ds(plane * SHIFT + u * DEPTH, DEPTH), :] = units[
                i, plane * X + u, 0:DEPTH
            ]
        columns = pl.ds(pl.multiple_of(plane * 512, 128), WINDOW)
        hi, lo = split(panel[plane])
        both = jnp.dot(
            high[:, columns], jnp.concatenate([hi, lo], axis=1), preferred_element_type=F32
        )
        rest = jnp.dot(low[:, columns], hi, preferred_element_type=F32)
        total[i] += both[:, 0:128] + (both[:, 128:256] + rest)

    def produce(i):
        some = tiles.at[i, pl.ds(0, PLANE - 1)]
        pltpu.make_async_copy(some, some, tile_recv.at[i]).wait()
        units[i, r] = jnp.transpose(tiles[i].reshape(128, 128))[0:UNIT]

        @pl.when(zh == 1)
        def _():
            across(i, r).start()

    def pass_on(i):
        bundle(i).wait_recv()
        send_tiles(i, relay, i * PLANE)

    def step(i, s, own):
        rights, lefts = (RIGHT_OWN, LEFT_OWN) if own else (RIGHT_OTHER, LEFT_OTHER)
        if s == 0:
            if not own:
                across(i, facing).wait_recv()
            hop(i, rights, 1).start()
            hop(i, lefts, 1).start()
            return [r if own else facing]
        got = []
        for lane, hops in ((rights, 4 if own else 3), (lefts, 3 if own else 4)):
            if s <= hops:
                got.append(land(i, lane, s))
                if s < hops:
                    hop(i, lane, s + 1).start()
        return got

    def core_copy(i):
        return pltpu.make_async_remote_copy(
            src_ref=partial.at[i, 1 - core],
            dst_ref=from_core.at[i],
            send_sem=core_send.at[i],
            recv_sem=core_recv.at[i],
            device_id=(r, zl * PLANE + y * 2 + 1 - core),
            device_id_type=MESH,
        )

    def sum_cores(i):
        ladder = jnp.transpose(total[i])
        for t in range(PLANE):
            partial[i, t % 2, t // 2] = ladder[8 * t : 8 * t + 8]
        core_copy(i).start()

    def sum_y(i):
        core_copy(i).wait_recv()
        partial[i, core] = partial[i, core] + from_core[i]

        def one(n, carry):
            t = (y + far_first(n, 8)) % 8
            pltpu.make_async_remote_copy(
                src_ref=partial.at[i, core, t],
                dst_ref=from_y.at[i, y],
                send_sem=y_send.at[i],
                recv_sem=y_recv.at[i],
                device_id=(r, zl * PLANE + t * 2 + core),
                device_id_type=MESH,
            ).start()
            return carry

        lax.fori_loop(0, 7, one, 0)
        from_y[i, y] = partial[i, core, y]

    def z_copy(i):
        return pltpu.make_async_remote_copy(
            src_ref=to_z.at[i],
            dst_ref=from_z.at[i],
            send_sem=z_send.at[i],
            recv_sem=z_recv.at[i],
            device_id=(r, ((zl + i) % STAGES) * PLANE + m),
            device_id_type=MESH,
        )

    def sum_z(i):
        seven = from_y.at[i, pl.ds(0, 7)]
        pltpu.make_async_copy(seven, seven, y_recv.at[i]).wait()
        value = from_y[i, 0]
        for j in range(1, 8):
            value = value + from_y[i, j]
        to_z[i] = value

    def drain(i):
        some = units.at[i, pl.ds(0, 15)]
        pltpu.make_async_copy(some, some, unit_send.at[i]).wait()
        some = tiles.at[i, pl.ds(0, PLANE - 1)]
        pltpu.make_async_copy(some, some, tile_send.at[i]).wait()
        core_copy(i).wait_send()
        some = from_y.at[i, pl.ds(0, 7)]
        pltpu.make_async_copy(some, some, y_send.at[i]).wait()

    def within(n):
        return (n >= 0) & (n < STAGES)

    def own_step(n, s):
        @pl.when((n - s >= 0) & (n - s < 2))
        def _():
            for b in range(2):
                step((n - s) * 2 + b, s, True)

    total[...] = jnp.zeros_like(total)
    panel[...] = jnp.zeros_like(panel)
    split_integrals()
    pass_on(1)
    produce(0)
    step(0, 0, True)
    pass_on(2)
    pass_on(3)
    produce(1)
    step(1, 0, True)
    produce(2)
    produce(3)

    def turn(n, carry):
        for s in (4, 3, 2, 1):
            own_step(n, s)

        @pl.when(n == 1)
        def _():
            step(2, 0, True)
            step(3, 0, True)

        for s in (4, 3, 2, 1, 0):

            @pl.when(within(n - 3 - s))
            def _(s=s):
                step(n - 3 - s, s, False)

        @pl.when((n == 2) & (zh == 0))
        def _():
            pl.semaphore_wait(facing_here, 1)
            for i in range(STAGES):
                across(i, r).start()

        @pl.when(n >= 8)
        def _():
            sum_y(n - 8)

        @pl.when(within(n - 4))
        def _():
            add(n - 4, zh)

        @pl.when(within(n - 7))
        def _():
            add(n - 7, 1 - zh)
            sum_cores(n - 7)

        @pl.when(n == 10)
        def _():
            sum_z(0)

        return carry

    lax.fori_loop(1, 11, turn, 0)

    last = STAGES - 1
    sum_y(last)
    for i in (1, 2):
        sum_z(i)
        z_copy(i).start()

    for load in loads[2:]:
        load.wait()
    pair = jnp.transpose(
        jnp.concatenate(
            [
                jnp.concatenate([pair_ref[...].astype(F32), jnp.zeros((2, 120), F32)], axis=1),
                jnp.zeros((126, 128), F32),
            ],
            axis=0,
        )
    )[0:8]
    table = lax.broadcasted_iota(jnp.int32, (8, 128), 1).astype(F32)
    occ = occ_ref[...].reshape(1, 128)
    occ_first = jnp.sum(jnp.where(pair[:, 0:1] == table, occ, 0.0), axis=1, keepdims=True)
    occ_second = jnp.sum(jnp.where(pair[:, 1:2] == table, occ, 0.0), axis=1, keepdims=True)
    vir = vir_ref[...].reshape(1, NV)
    blocks = lax.broadcasted_iota(jnp.int32, (1, 8), 1)
    a_pick = jnp.sum(
        jnp.where(blocks == r // 2, aorb_ref[...].astype(F32).reshape(1, 8), 0.0),
        axis=1,
        keepdims=True,
    )
    orbitals = lax.broadcasted_iota(jnp.int32, (1, NV), 1).astype(F32)
    vir_a = jnp.sum(jnp.where(orbitals == a_pick, vir, 0.0), axis=1, keepdims=True)
    vir_b = jnp.where(r % 2 == 0, vir[:, 0:AB], vir[:, AB:NV])
    denom = (occ_first + occ_second) - (vir_a + vir_b)

    for i in range(1, STAGES):
        bundle(i).wait_send()
    for i in range(STAGES):
        drain(i)
    sum_z(last)
    z_copy(last).start()
    ladder = to_z[0]
    for i in range(1, STAGES):
        z_copy(i).wait_recv()
        ladder = ladder + from_z[i]
    out_ref[...] = old_ref[...] + (ladder[:, 0:AB] + other_ref[...]) / denom
    for i in range(1, STAGES):
        z_copy(i).wait_send()


def local(
    integrals, amplitudes, old_amps, other_terms, occ_energy, vir_energy, pair_occ, a_orbitals
):
    vmem = pl.BlockSpec(memory_space=pltpu.VMEM)
    dma = pltpu.SemaphoreType.DMA
    return pl.pallas_call(
        kernel,
        out_shape=jax.ShapeDtypeStruct((8, AB), F32),
        in_specs=[pl.BlockSpec(memory_space=pltpu.HBM)] * 8,
        out_specs=vmem,
        scratch_shapes=[
            pltpu.VMEM((AB, NV), F32),
            pltpu.VMEM((8 * 64, DEPTH), F32),
            pltpu.VMEM((8, AB), F32),
            pltpu.VMEM((8, AB), F32),
            pltpu.VMEM((128,), F32),
            pltpu.VMEM((NV,), F32),
            pltpu.VMEM((2, 8), jnp.int32),
            pltpu.VMEM((8,), jnp.int32),
            pltpu.VMEM((64, 8, 128), F32),
            pltpu.VMEM((64, 8, 128), F32),
            pltpu.VMEM((STAGES, PLANE, 8, 128), F32),
            pltpu.VMEM((STAGES, ROWS, UNIT, 128), F32),
            pltpu.VMEM((ABP, NVP), BF16),
            pltpu.VMEM((ABP, NVP), BF16),
            pltpu.VMEM((2, WINDOW, 128), F32),
            pltpu.VMEM((STAGES, ABP, 128), F32),
            pltpu.VMEM((STAGES, 2, 8, 8, ABP), F32),
            pltpu.VMEM((STAGES, 8, 8, ABP), F32),
            pltpu.VMEM((STAGES, 8, 8, ABP), F32),
            pltpu.VMEM((STAGES, 8, ABP), F32),
            pltpu.VMEM((STAGES, 8, ABP), F32),
            pltpu.SemaphoreType.REGULAR,
            dma((8,)),
            dma((STAGES,)),
            dma((STAGES,)),
            dma((STAGES,)),
            dma((STAGES,)),
            dma((STAGES,)),
            dma((STAGES, 15)),
            dma((STAGES,)),
            dma((STAGES,)),
            dma((STAGES,)),
            dma((STAGES,)),
            dma((STAGES,)),
            dma((STAGES,)),
        ],
        compiler_params=pltpu.CompilerParams(
            collective_id=0, has_side_effects=True, vmem_limit_bytes=60 * 1024 * 1024
        ),
        cost_estimate=pl.CostEstimate(
            flops=6 * 512 * AB * NV, bytes_accessed=4 * AB * NV, transcendentals=0
        ),
    )(
        integrals,
        amplitudes.reshape(8 * 64, DEPTH),
        old_amps,
        other_terms,
        occ_energy,
        vir_energy,
        pair_occ.T,
        a_orbitals,
    )


def solution(mesh):
    in_specs = (
        P("row", "col"),
        P("col", None, "row"),
        P("col", "row"),
        P("col", "row"),
        P(),
        P(),
        P("col", None),
        P(),
    )
    out_specs = P("col", "row")
    return jax.shard_map(local, mesh=mesh, in_specs=in_specs, out_specs=out_specs, check_vma=False)
```

```python
import jax
import jax.numpy as jnp
from jax import lax
from jax.experimental import pallas as pl
from jax.experimental.pallas import tpu as pltpu
from jax.sharding import PartitionSpec as P

NV = 1200
MESH = pl.DeviceIdType.MESH
X = 8
PLANE = 16
STAGES = 4
ROWS = 16
OTHER_TURN = 2
DEPTH = 75
UNIT = 80
AB = 600
ABP = 640
NVP = 1280
WINDOW = 768
SHIFT = 88
F32 = jnp.float32
BF16 = jnp.bfloat16

OWN_LONG, OWN_SHORT, OTHER_LONG, OTHER_SHORT = 0, 4, 7, 11


def far_first(n, count):
    return count // 2 + (n + 1) // 2 * (1 - 2 * (n % 2))


def kernel(
    integrals_hbm,
    amps_hbm,
    old_hbm,
    other_hbm,
    occ_hbm,
    vir_hbm,
    pair_hbm,
    aorb_hbm,
    out_ref,
    integ,
    amps_ref,
    old_ref,
    other_ref,
    occ_ref,
    vir_ref,
    pair_ref,
    aorb_ref,
    near_out,
    near_in,
    far_out,
    far_in,
    units_out,
    units,
    high,
    low,
    panel,
    total,
    partial,
    from_core,
    join,
    from_y,
    to_z,
    from_z,
    half_here,
    facing_here,
    load_sem,
    near_send,
    near_recv,
    far_send,
    far_recv,
    up_send,
    up_recv,
    unit_send,
    unit_recv,
    core_send,
    core_recv,
    join_recv,
    y_send,
    y_recv,
    z_send,
    z_recv,
):
    r = lax.axis_index("row")
    k = lax.axis_index("col")
    x, zh = r % X, r // X
    zl, m = k // PLANE, k % PLANE
    y, core = m // 2, m % 2
    right = zh * X + (x + 1) % X
    left = zh * X + (x + X - 1) % X
    facing = (r + X) % ROWS

    loads = [
        pltpu.make_async_copy(source, target, load_sem.at[n])
        for n, (source, target) in enumerate(
            (
                (amps_hbm, amps_ref),
                (integrals_hbm, integ),
                (old_hbm, old_ref),
                (other_hbm, other_ref),
                (occ_hbm, occ_ref),
                (vir_hbm, vir_ref),
                (pair_hbm, pair_ref),
                (aorb_hbm, aorb_ref),
            )
        )
    ]
    loads[0].start()

    barrier = pltpu.get_barrier_semaphore()

    def greet(row, col):
        pl.semaphore_signal(barrier, inc=1, device_id=(row, col), device_id_type=MESH)

    def greet_plane(j, carry):
        greet(r, zl * PLANE + (m + j) % PLANE)
        return carry

    lax.fori_loop(1, PLANE, greet_plane, 0)
    greet(right, k)
    greet(left, k)

    for j in range(1, STAGES):

        @pl.when(zl + j < STAGES)
        def _(j=j):
            greet(r, k + j * PLANE)

    @pl.when(zh == 0)
    def _():
        for j in range(STAGES):
            greet(facing, j * PLANE + m)

    def tile_of(plane, t):
        return amps_ref[pl.ds(plane % STAGES * PLANE + t, 8, stride=64), :]

    near_out[...] = jnp.zeros_like(near_out)
    far_out[...] = jnp.zeros_like(far_out)
    loads[0].wait()
    for load in loads[1:]:
        load.start()
    for t in range(PLANE):
        near_out[t, :, 0:DEPTH] = tile_of(zl, t)
    pl.semaphore_wait(barrier, PLANE - 1 + 2 + zl + STAGES * zh)

    def answer(sem, row, col):
        pl.semaphore_signal(sem, inc=1, device_id=(row, col), device_id_type=MESH)

    for j in range(1, STAGES):

        @pl.when(zl >= j)
        def _(j=j):
            answer(half_here, r, k - j * PLANE)

    @pl.when(zh == 1)
    def _():
        for j in range(STAGES):
            answer(facing_here, facing, j * PLANE + m)

    def send_tiles(source, target, send_sem, recv_sem):
        def one(n, carry):
            t = (m + far_first(n, PLANE)) % PLANE
            pltpu.make_async_remote_copy(
                src_ref=source.at[t],
                dst_ref=target.at[m],
                send_sem=send_sem,
                recv_sem=recv_sem,
                device_id=(r, zl * PLANE + t),
                device_id_type=MESH,
            ).start()
            return carry

        lax.fori_loop(0, PLANE - 1, one, 0)
        target[m] = source[m]

    def wait_for(some, sem):
        pltpu.make_async_copy(some, some, sem).wait()

    send_tiles(near_out, near_in, near_send, near_recv)
    for t in range(PLANE):
        for q in range(STAGES - 1):
            far_out[t, :, q * DEPTH : (q + 1) * DEPTH] = tile_of(zl + 1 + q, t)
    send_tiles(far_out, far_in, far_send, far_recv)

    def split(v):
        hi = v.astype(BF16)
        return hi, (v - hi.astype(F32)).astype(BF16)

    def split_integrals():
        loads[1].wait()
        last = NV // 128 * 128
        for part in (high, low):
            part[:, last:] = jnp.zeros((ABP, NVP - last), BF16)

        def chunk(n, carry):
            rows = pl.ds(pl.multiple_of(n * 128, 128), 128)
            hi, lo = split(integ[rows, :])
            high[rows, 0:NV] = hi
            low[rows, 0:NV] = lo
            return carry

        lax.fori_loop(0, 4, chunk, 0)
        pad = jnp.zeros((ABP - AB, NV), BF16)
        hi, lo = split(integ[512:AB, :])
        high[512:ABP, 0:NV] = jnp.concatenate([hi, pad], axis=0)
        low[512:ABP, 0:NV] = jnp.concatenate([lo, pad], axis=0)

    def way(i, lane):
        sign = 1 if lane in (OWN_LONG, OTHER_SHORT) else -1
        return sign * (1 - 2 * (i % 2))

    def copy_unit(i, lane, h, origin):
        return pltpu.make_async_remote_copy(
            src_ref=units.at[i, origin],
            dst_ref=units.at[i, origin],
            send_sem=unit_send.at[i],
            recv_sem=unit_recv.at[i, lane + h],
            device_id=(zh * X + (x + X + way(i, lane)) % X, k),
            device_id_type=MESH,
        )

    def origin_of(i, lane, h):
        plane = zh if lane in (OWN_LONG, OWN_SHORT) else 1 - zh
        return plane * X + (x + X - h * way(i, lane)) % X

    def hop(i, lane, h):
        return copy_unit(i, lane, h, origin_of(i, lane, h - 1))

    def land(i, lane, h):
        copy_unit(i, lane, h, origin_of(i, lane, h)).wait_recv()

    def add(i, plane):
        for u in range(X):
            panel[plane, pl.ds(plane * SHIFT + u * DEPTH, DEPTH), :] = units[
                i, plane * X + u, 0:DEPTH
            ]
        columns = pl.ds(pl.multiple_of(plane * 512, 128), WINDOW)
        hi, lo = split(panel[plane])
        both = jnp.dot(
            high[:, columns], jnp.concatenate([hi, lo], axis=1), preferred_element_type=F32
        )
        rest = jnp.dot(low[:, columns], hi, preferred_element_type=F32)
        total[i] += both[:, 0:128] + (both[:, 128:256] + rest)

    def unit_to(source, plane, row, recv_sem):
        return pltpu.make_async_remote_copy(
            src_ref=source,
            dst_ref=units.at[zl, r],
            send_sem=up_send,
            recv_sem=recv_sem,
            device_id=(row, plane * PLANE + m),
            device_id_type=MESH,
        )

    def to_half():
        for q in range(STAGES - 1):
            unit_to(units_out.at[q], (zl + 1 + q) % STAGES, r, up_recv.at[zl]).start()

    def to_facing():
        arrived = unit_recv.at[zl, 0]
        unit_to(units.at[zl, r], zl, facing, arrived).start()
        for q in range(STAGES - 1):
            unit_to(units_out.at[q], (zl + 1 + q) % STAGES, facing, arrived).start()

    def begin(i):
        @pl.when(zl != i)
        def _():
            wait_for(units.at[i, r], up_recv.at[i])

        step(i, 0, True)

    def make_units():
        wait_for(near_in.at[pl.ds(0, PLANE - 1)], near_recv)
        units[zl, r] = jnp.transpose(near_in[...].reshape(128, 128))[0:UNIT]
        wait_for(far_in.at[pl.ds(0, PLANE - 1)], far_recv)
        turned = jnp.transpose(far_in[...].reshape(128, 256))
        for q in range(STAGES - 1):
            units_out[q] = turned[q * DEPTH : q * DEPTH + UNIT]

    def step(i, s, own):
        long, short = (OWN_LONG, OWN_SHORT) if own else (OTHER_LONG, OTHER_SHORT)
        if s == 0 and not own:
            wait_for(units.at[i, facing], unit_recv.at[i, 0])
        for lane, hops in ((long, 4), (short, 3)):
            if 1 <= s <= hops:
                land(i, lane, s)
            if s < hops:
                hop(i, lane, s + 1).start()

    def core_copy(i):
        return pltpu.make_async_remote_copy(
            src_ref=partial.at[i, 1 - core],
            dst_ref=from_core.at[i],
            send_sem=core_send.at[i],
            recv_sem=core_recv.at[i],
            device_id=(r, zl * PLANE + y * 2 + 1 - core),
            device_id_type=MESH,
        )

    def sum_cores(i):
        ladder = jnp.transpose(total[i])
        for t in range(PLANE):
            partial[i, t % 2, t // 2] = ladder[8 * t : 8 * t + 8]
        core_copy(i).start()

    def y_copy(i, block, away, target, recv_sem):
        return pltpu.make_async_remote_copy(
            src_ref=partial.at[i, core, (y + 8 + block) % 8],
            dst_ref=target,
            send_sem=y_send.at[i],
            recv_sem=recv_sem,
            device_id=(r, zl * PLANE + (y + 8 + away) % 8 * 2 + core),
            device_id_type=MESH,
        )

    def sum_y(i):
        core_copy(i).wait_recv()
        partial[i, core] = partial[i, core] + from_core[i]
        y_copy(i, 4, 2 - 4 * (i % 2), join.at[i, 2], join_recv.at[i]).start()
        for n, side in enumerate((1, -1)):
            y_copy(i, 3 * side, side, join.at[i, n], join_recv.at[i]).start()
        for n, side in enumerate((1, -1)):
            y_copy(i, side, side, from_y.at[i, n], y_recv.at[i]).start()

    def join_y(i):
        wait_for(join.at[i], join_recv.at[i])
        for n, away in enumerate((2, -2, 2 - 4 * (i % 2))):
            block = (y + 8 + away) % 8
            partial[i, core, block] = partial[i, core, block] + join[i, n]
        for n, side in enumerate((2, -2)):
            y_copy(i, side, side, from_y.at[i, 2 + n], y_recv.at[i]).start()

    def z_copy(i):
        return pltpu.make_async_remote_copy(
            src_ref=to_z.at[i],
            dst_ref=from_z.at[zl],
            send_sem=z_send.at[i],
            recv_sem=z_recv.at[zl],
            device_id=(r, i * PLANE + m),
            device_id_type=MESH,
        )

    def sum_z(i):
        wait_for(from_y.at[i], y_recv.at[i])
        value = partial[i, core, y]
        for j in range(4):
            value = value + from_y[i, j]
        to_z[i] = value

    def give(i):
        @pl.when(zl != i)
        def _():
            z_copy(i).start()

    def drain(i):
        wait_for(units.at[i, pl.ds(0, 14)], unit_send.at[i])
        core_copy(i).wait_send()
        wait_for(partial.at[i, 0, pl.ds(0, 7)], y_send.at[i])

    def pair_step(n, first, s, own):
        @pl.when((n - first - s >= 0) & (n - first - s < 2))
        def _():
            for b in range(2):
                step((n - first - s) * 2 + b, s, own)

    total[...] = jnp.zeros_like(total)
    panel[...] = jnp.zeros_like(panel)
    split_integrals()
    make_units()

    @pl.when(zl < STAGES - 1)
    def _():
        pl.semaphore_wait(half_here, STAGES - 1 - zl)

    to_half()

    @pl.when(zh == 1)
    def _():
        to_facing()

    for i in range(STAGES):
        begin(i)

    def turn(n, carry):
        for s in (4, 3, 2, 1):

            @pl.when(n == s)
            def _(s=s):
                for i in range(STAGES):
                    step(i, s, True)

        for s in (4, 3, 2, 1, 0):
            pair_step(n, OTHER_TURN, s, False)

        @pl.when((n == 1) & (zh == 0))
        def _():
            pl.semaphore_wait(facing_here, STAGES)
            to_facing()

        @pl.when((n == OTHER_TURN + 2) | (n == OTHER_TURN + 3))
        def _():
            for b in range(2):
                add((n - OTHER_TURN - 2) * 2 + b, zh)

        return carry

    lax.fori_loop(1, OTHER_TURN + 4, turn, 0)
    for i in range(STAGES):
        step(i, 4 - i // 2, False)
    for i in (0, 1):
        add(i, 1 - zh)
        sum_cores(i)
    for i in (0, 1):
        sum_y(i)
    for i in (2, 3):
        step(i, 4, False)
        add(i, 1 - zh)
        sum_cores(i)
    for i in (0, 1):
        join_y(i)
    for i in (2, 3):
        sum_y(i)
    for i in (0, 1):
        sum_z(i)
        give(i)
    for i in (2, 3):
        join_y(i)

    for load in loads[2:]:
        load.wait()
    pair = jnp.transpose(
        jnp.concatenate(
            [
                jnp.concatenate([pair_ref[...].astype(F32), jnp.zeros((2, 120), F32)], axis=1),
                jnp.zeros((126, 128), F32),
            ],
            axis=0,
        )
    )[0:8]
    table = lax.broadcasted_iota(jnp.int32, (8, 128), 1).astype(F32)
    occ = occ_ref[...].reshape(1, 128)
    occ_first = jnp.sum(jnp.where(pair[:, 0:1] == table, occ, 0.0), axis=1, keepdims=True)
    occ_second = jnp.sum(jnp.where(pair[:, 1:2] == table, occ, 0.0), axis=1, keepdims=True)
    vir = vir_ref[...].reshape(1, NV)
    blocks = lax.broadcasted_iota(jnp.int32, (1, 8), 1)
    a_pick = jnp.sum(
        jnp.where(blocks == r // 2, aorb_ref[...].astype(F32).reshape(1, 8), 0.0),
        axis=1,
        keepdims=True,
    )
    orbitals = lax.broadcasted_iota(jnp.int32, (1, NV), 1).astype(F32)
    vir_a = jnp.sum(jnp.where(orbitals == a_pick, vir, 0.0), axis=1, keepdims=True)
    vir_b = jnp.where(r % 2 == 0, vir[:, 0:AB], vir[:, AB:NV])
    denom = (occ_first + occ_second) - (vir_a + vir_b)

    wait_for(near_in.at[pl.ds(0, PLANE - 1)], near_send)
    wait_for(far_in.at[pl.ds(0, PLANE - 1)], far_send)
    wait_for(units.at[0, pl.ds(0, 7)], up_send)
    for i in range(STAGES):
        drain(i)
    for i in (2, 3):
        sum_z(i)
        give(i)
    others = other_ref[...]
    for q in range(STAGES - 1):
        source = (zl + 1 + q) % STAGES
        wait_for(from_z.at[source], z_recv.at[source])
        others = others + from_z[source, :, 0:AB]
    out_ref[...] = old_ref[...] + (to_z[zl, :, 0:AB] + others) / denom
    for i in range(STAGES):

        @pl.when(zl != i)
        def _(i=i):
            z_copy(i).wait_send()


def local(
    integrals, amplitudes, old_amps, other_terms, occ_energy, vir_energy, pair_occ, a_orbitals
):
    vmem = pl.BlockSpec(memory_space=pltpu.VMEM)
    dma = pltpu.SemaphoreType.DMA
    return pl.pallas_call(
        kernel,
        out_shape=jax.ShapeDtypeStruct((8, AB), F32),
        in_specs=[pl.BlockSpec(memory_space=pltpu.HBM)] * 8,
        out_specs=vmem,
        scratch_shapes=[
            pltpu.VMEM((AB, NV), F32),
            pltpu.VMEM((8 * 64, DEPTH), F32),
            pltpu.VMEM((8, AB), F32),
            pltpu.VMEM((8, AB), F32),
            pltpu.VMEM((128,), F32),
            pltpu.VMEM((NV,), F32),
            pltpu.VMEM((2, 8), jnp.int32),
            pltpu.VMEM((8,), jnp.int32),
            pltpu.VMEM((PLANE, 8, 128), F32),
            pltpu.VMEM((PLANE, 8, 128), F32),
            pltpu.VMEM((PLANE, 8, 256), F32),
            pltpu.VMEM((PLANE, 8, 256), F32),
            pltpu.VMEM((STAGES - 1, UNIT, 128), F32),
            pltpu.VMEM((STAGES, ROWS, UNIT, 128), F32),
            pltpu.VMEM((ABP, NVP), BF16),
            pltpu.VMEM((ABP, NVP), BF16),
            pltpu.VMEM((2, WINDOW, 128), F32),
            pltpu.VMEM((STAGES, ABP, 128), F32),
            pltpu.VMEM((STAGES, 2, 8, 8, ABP), F32),
            pltpu.VMEM((STAGES, 8, 8, ABP), F32),
            pltpu.VMEM((STAGES, 3, 8, ABP), F32),
            pltpu.VMEM((STAGES, 4, 8, ABP), F32),
            pltpu.VMEM((STAGES, 8, ABP), F32),
            pltpu.VMEM((STAGES, 8, ABP), F32),
            pltpu.SemaphoreType.REGULAR,
            pltpu.SemaphoreType.REGULAR,
            dma((8,)),
            dma,
            dma,
            dma,
            dma,
            dma,
            dma((STAGES,)),
            dma((STAGES,)),
            dma((STAGES, 15)),
            dma((STAGES,)),
            dma((STAGES,)),
            dma((STAGES,)),
            dma((STAGES,)),
            dma((STAGES,)),
            dma((STAGES,)),
            dma((STAGES,)),
        ],
        compiler_params=pltpu.CompilerParams(
            collective_id=0, has_side_effects=True, vmem_limit_bytes=60 * 1024 * 1024
        ),
        cost_estimate=pl.CostEstimate(
            flops=6 * 512 * AB * NV, bytes_accessed=4 * AB * NV, transcendentals=0
        ),
    )(
        integrals,
        amplitudes.reshape(8 * 64, DEPTH),
        old_amps,
        other_terms,
        occ_energy,
        vir_energy,
        pair_occ.T,
        a_orbitals,
    )


def solution(mesh):
    in_specs = (
        P("row", "col"),
        P("col", None, "row"),
        P("col", "row"),
        P("col", "row"),
        P(),
        P(),
        P("col", None),
        P(),
    )
    out_specs = P("col", "row")
    return jax.shard_map(local, mesh=mesh, in_specs=in_specs, out_specs=out_specs, check_vma=False)
```

```python
import jax
import jax.numpy as jnp
from jax import lax
from jax.experimental import pallas as pl
from jax.experimental.pallas import tpu as pltpu
from jax.sharding import PartitionSpec as P

NV = 1200
MESH = pl.DeviceIdType.MESH
X = 8
PLANE = 16
STAGES = 4
ROWS = 16
OTHER_TURN = 2
DEPTH = 75
UNIT = 80
AB = 600
ABP = 640
NVP = 1280
WINDOW = 768
SHIFT = 88
F32 = jnp.float32
BF16 = jnp.bfloat16

OWN_LONG, OWN_SHORT, OTHER_LONG, OTHER_SHORT = 0, 4, 7, 11


def far_first(n, count):
    return count // 2 + (n + 1) // 2 * (1 - 2 * (n % 2))


def kernel(
    integrals_hbm,
    amps_hbm,
    old_hbm,
    other_hbm,
    occ_hbm,
    vir_hbm,
    pair_hbm,
    aorb_hbm,
    out_ref,
    integ,
    amps_ref,
    old_ref,
    other_ref,
    occ_ref,
    vir_ref,
    pair_ref,
    aorb_ref,
    near_out,
    near_in,
    far_out,
    far_in,
    units_out,
    units,
    high,
    low,
    panel,
    last_panel,
    total,
    partial,
    from_core,
    join,
    from_y,
    to_z,
    from_z,
    half_here,
    facing_here,
    load_sem,
    near_send,
    near_recv,
    far_send,
    far_recv,
    up_send,
    up_recv,
    unit_send,
    unit_recv,
    core_send,
    core_recv,
    join_recv,
    y_send,
    y_recv,
    z_send,
    z_recv,
):
    r = lax.axis_index("row")
    k = lax.axis_index("col")
    x, zh = r % X, r // X
    zl, m = k // PLANE, k % PLANE
    y, core = m // 2, m % 2
    right = zh * X + (x + 1) % X
    left = zh * X + (x + X - 1) % X
    facing = (r + X) % ROWS

    loads = [
        pltpu.make_async_copy(source, target, load_sem.at[n])
        for n, (source, target) in enumerate(
            (
                (amps_hbm, amps_ref),
                (integrals_hbm, integ),
                (old_hbm, old_ref),
                (other_hbm, other_ref),
                (occ_hbm, occ_ref),
                (vir_hbm, vir_ref),
                (pair_hbm, pair_ref),
                (aorb_hbm, aorb_ref),
            )
        )
    ]
    loads[0].start()

    barrier = pltpu.get_barrier_semaphore()

    def greet(row, col):
        pl.semaphore_signal(barrier, inc=1, device_id=(row, col), device_id_type=MESH)

    def greet_plane(j, carry):
        greet(r, zl * PLANE + (m + j) % PLANE)
        return carry

    lax.fori_loop(1, PLANE, greet_plane, 0)
    greet(right, k)
    greet(left, k)

    for j in range(1, STAGES):

        @pl.when(zl + j < STAGES)
        def _(j=j):
            greet(r, k + j * PLANE)

    @pl.when(zh == 0)
    def _():
        for j in range(STAGES):
            greet(facing, j * PLANE + m)

    def tile_of(plane, t):
        return amps_ref[pl.ds(plane % STAGES * PLANE + t, 8, stride=64), :]

    near_out[...] = jnp.zeros_like(near_out)
    far_out[...] = jnp.zeros_like(far_out)
    loads[0].wait()
    for load in loads[1:]:
        load.start()
    for t in range(PLANE):
        near_out[t, :, 0:DEPTH] = tile_of(zl, t)
    pl.semaphore_wait(barrier, PLANE - 1 + 2 + zl + STAGES * zh)

    def answer(sem, row, col):
        pl.semaphore_signal(sem, inc=1, device_id=(row, col), device_id_type=MESH)

    for j in range(1, STAGES):

        @pl.when(zl >= j)
        def _(j=j):
            answer(half_here, r, k - j * PLANE)

    @pl.when(zh == 1)
    def _():
        for j in range(STAGES):
            answer(facing_here, facing, j * PLANE + m)

    def send_tiles(source, target, send_sem, recv_sem):
        def one(n, carry):
            t = (m + far_first(n, PLANE)) % PLANE
            pltpu.make_async_remote_copy(
                src_ref=source.at[t],
                dst_ref=target.at[m],
                send_sem=send_sem,
                recv_sem=recv_sem,
                device_id=(r, zl * PLANE + t),
                device_id_type=MESH,
            ).start()
            return carry

        lax.fori_loop(0, PLANE - 1, one, 0)
        target[m] = source[m]

    def wait_for(some, sem):
        pltpu.make_async_copy(some, some, sem).wait()

    send_tiles(near_out, near_in, near_send, near_recv)
    for t in range(PLANE):
        for q in range(STAGES - 1):
            far_out[t, :, q * DEPTH : (q + 1) * DEPTH] = tile_of(zl + 1 + q, t)
    send_tiles(far_out, far_in, far_send, far_recv)

    def split(v):
        hi = v.astype(BF16)
        return hi, (v - hi.astype(F32)).astype(BF16)

    def split_integrals():
        loads[1].wait()
        last = NV // 128 * 128
        for part in (high, low):
            part[:, last:] = jnp.zeros((ABP, NVP - last), BF16)

        def chunk(n, carry):
            rows = pl.ds(pl.multiple_of(n * 128, 128), 128)
            hi, lo = split(integ[rows, :])
            high[rows, 0:NV] = hi
            low[rows, 0:NV] = lo
            return carry

        lax.fori_loop(0, 4, chunk, 0)
        pad = jnp.zeros((ABP - AB, NV), BF16)
        hi, lo = split(integ[512:AB, :])
        high[512:ABP, 0:NV] = jnp.concatenate([hi, pad], axis=0)
        low[512:ABP, 0:NV] = jnp.concatenate([lo, pad], axis=0)

    def way(i, lane):
        sign = 1 if lane in (OWN_LONG, OTHER_SHORT) else -1
        return sign * (1 - 2 * (i % 2))

    def copy_unit(i, lane, h, origin):
        return pltpu.make_async_remote_copy(
            src_ref=units.at[i, origin],
            dst_ref=units.at[i, origin],
            send_sem=unit_send.at[i],
            recv_sem=unit_recv.at[i, lane + h],
            device_id=(zh * X + (x + X + way(i, lane)) % X, k),
            device_id_type=MESH,
        )

    def origin_of(i, lane, h):
        plane = zh if lane in (OWN_LONG, OWN_SHORT) else 1 - zh
        return plane * X + (x + X - h * way(i, lane)) % X

    def hop(i, lane, h):
        return copy_unit(i, lane, h, origin_of(i, lane, h - 1))

    def land(i, lane, h):
        copy_unit(i, lane, h, origin_of(i, lane, h)).wait_recv()

    def multiply(i, start, width, units_here):
        columns = pl.ds(pl.multiple_of(start, 128), width)
        hi, lo = split(units_here)
        both = jnp.dot(
            high[:, columns], jnp.concatenate([hi, lo], axis=1), preferred_element_type=F32
        )
        rest = jnp.dot(low[:, columns], hi, preferred_element_type=F32)
        total[i] += both[:, 0:128] + (both[:, 128:256] + rest)

    def place(i, plane, u):
        panel[plane, pl.ds(plane * SHIFT + u * DEPTH, DEPTH), :] = units[i, plane * X + u, 0:DEPTH]

    def add(i, plane):
        for u in range(X):
            place(i, plane, u)
        multiply(i, plane * 512, WINDOW, panel[plane])

    other, farthest = 1 - zh, (x + X // 2) % X
    last_row = other * SHIFT + farthest * DEPTH

    def add_first(i):
        for n in range(1, X):
            place(i, other, (farthest + n) % X)
        panel[other, pl.ds(last_row, DEPTH), :] = jnp.zeros((DEPTH, 128), F32)
        multiply(i, other * 512, WINDOW, panel[other])

    def add_last(i):
        last_panel[pl.ds(last_row % 128, DEPTH), :] = units[i, other * X + farthest, 0:DEPTH]
        multiply(i, other * 512 + last_row // 128 * 128, 256, last_panel[...])

    def unit_to(source, plane, row, recv_sem):
        return pltpu.make_async_remote_copy(
            src_ref=source,
            dst_ref=units.at[zl, r],
            send_sem=up_send,
            recv_sem=recv_sem,
            device_id=(row, plane * PLANE + m),
            device_id_type=MESH,
        )

    def to_half():
        for q in range(STAGES - 1):
            unit_to(units_out.at[q], (zl + 1 + q) % STAGES, r, up_recv.at[zl]).start()

    def to_facing():
        arrived = unit_recv.at[zl, 0]
        unit_to(units.at[zl, r], zl, facing, arrived).start()
        for q in range(STAGES - 1):
            unit_to(units_out.at[q], (zl + 1 + q) % STAGES, facing, arrived).start()

    def begin(i):
        @pl.when(zl != i)
        def _():
            wait_for(units.at[i, r], up_recv.at[i])

        step(i, 0, True)

    def make_units():
        wait_for(near_in.at[pl.ds(0, PLANE - 1)], near_recv)
        units[zl, r] = jnp.transpose(near_in[...].reshape(128, 128))[0:UNIT]
        wait_for(far_in.at[pl.ds(0, PLANE - 1)], far_recv)
        turned = jnp.transpose(far_in[...].reshape(128, 256))
        for q in range(STAGES - 1):
            units_out[q] = turned[q * DEPTH : q * DEPTH + UNIT]

    def step(i, s, own):
        long, short = (OWN_LONG, OWN_SHORT) if own else (OTHER_LONG, OTHER_SHORT)
        if s == 0 and not own:
            wait_for(units.at[i, facing], unit_recv.at[i, 0])
        for lane, hops in ((long, 4), (short, 3)):
            if 1 <= s <= hops:
                land(i, lane, s)
            if s < hops:
                hop(i, lane, s + 1).start()

    def core_copy(i):
        return pltpu.make_async_remote_copy(
            src_ref=partial.at[i, 1 - core],
            dst_ref=from_core.at[i],
            send_sem=core_send.at[i],
            recv_sem=core_recv.at[i],
            device_id=(r, zl * PLANE + y * 2 + 1 - core),
            device_id_type=MESH,
        )

    def sum_cores(i):
        ladder = jnp.transpose(total[i])
        for t in range(PLANE):
            partial[i, t % 2, t // 2] = ladder[8 * t : 8 * t + 8]
        core_copy(i).start()

    def y_copy(i, block, away, target, recv_sem):
        return pltpu.make_async_remote_copy(
            src_ref=partial.at[i, core, (y + 8 + block) % 8],
            dst_ref=target,
            send_sem=y_send.at[i],
            recv_sem=recv_sem,
            device_id=(r, zl * PLANE + (y + 8 + away) % 8 * 2 + core),
            device_id_type=MESH,
        )

    def sum_y(i):
        core_copy(i).wait_recv()
        partial[i, core] = partial[i, core] + from_core[i]
        y_copy(i, 4, 2 - 4 * (i % 2), join.at[i, 2], join_recv.at[i]).start()
        for n, side in enumerate((1, -1)):
            y_copy(i, 3 * side, side, join.at[i, n], join_recv.at[i]).start()
        for n, side in enumerate((1, -1)):
            y_copy(i, side, side, from_y.at[i, n], y_recv.at[i]).start()

    def join_y(i):
        wait_for(join.at[i], join_recv.at[i])
        for n, away in enumerate((2, -2, 2 - 4 * (i % 2))):
            block = (y + 8 + away) % 8
            partial[i, core, block] = partial[i, core, block] + join[i, n]
        for n, side in enumerate((2, -2)):
            y_copy(i, side, side, from_y.at[i, 2 + n], y_recv.at[i]).start()

    def z_copy(i):
        return pltpu.make_async_remote_copy(
            src_ref=to_z.at[i],
            dst_ref=from_z.at[zl],
            send_sem=z_send.at[i],
            recv_sem=z_recv.at[zl],
            device_id=(r, i * PLANE + m),
            device_id_type=MESH,
        )

    def sum_z(i):
        wait_for(from_y.at[i], y_recv.at[i])
        value = partial[i, core, y]
        for j in range(4):
            value = value + from_y[i, j]
        to_z[i] = value

    def give(i):
        @pl.when(zl != i)
        def _():
            z_copy(i).start()

    def drain(i):
        wait_for(units.at[i, pl.ds(0, 14)], unit_send.at[i])
        core_copy(i).wait_send()
        wait_for(partial.at[i, 0, pl.ds(0, 7)], y_send.at[i])

    def pair_step(n, first, s, own):
        @pl.when((n - first - s >= 0) & (n - first - s < 2))
        def _():
            for b in range(2):
                step((n - first - s) * 2 + b, s, own)

    total[...] = jnp.zeros_like(total)
    panel[...] = jnp.zeros_like(panel)
    last_panel[...] = jnp.zeros_like(last_panel)
    split_integrals()
    make_units()

    @pl.when(zl < STAGES - 1)
    def _():
        pl.semaphore_wait(half_here, STAGES - 1 - zl)

    to_half()

    @pl.when(zh == 1)
    def _():
        to_facing()

    for i in range(STAGES):
        begin(i)

    def turn(n, carry):
        for s in (4, 3, 2, 1):

            @pl.when(n == s)
            def _(s=s):
                for i in range(STAGES):
                    step(i, s, True)

        for s in (4, 3, 2, 1, 0):
            pair_step(n, OTHER_TURN, s, False)

        @pl.when((n == 1) & (zh == 0))
        def _():
            pl.semaphore_wait(facing_here, STAGES)
            to_facing()

        @pl.when((n == OTHER_TURN + 2) | (n == OTHER_TURN + 3))
        def _():
            for b in range(2):
                add((n - OTHER_TURN - 2) * 2 + b, zh)

        @pl.when(n == OTHER_TURN + 3)
        def _():
            add_first(0)
            add_first(1)

        return carry

    lax.fori_loop(1, OTHER_TURN + 4, turn, 0)
    for i in range(STAGES):
        step(i, 4 - i // 2, False)
    for i in (0, 1):
        add_last(i)
        sum_cores(i)
    for i in (2, 3):
        add_first(i)
    for i in (0, 1):
        sum_y(i)
    for i in (2, 3):
        step(i, 4, False)
        add_last(i)
        sum_cores(i)
    for i in (0, 1):
        join_y(i)
    for i in (2, 3):
        sum_y(i)
    for i in (0, 1):
        sum_z(i)
        give(i)
    for i in (2, 3):
        join_y(i)

    for load in loads[2:]:
        load.wait()
    pair = jnp.transpose(
        jnp.concatenate(
            [
                jnp.concatenate([pair_ref[...].astype(F32), jnp.zeros((2, 120), F32)], axis=1),
                jnp.zeros((126, 128), F32),
            ],
            axis=0,
        )
    )[0:8]
    table = lax.broadcasted_iota(jnp.int32, (8, 128), 1).astype(F32)
    occ = occ_ref[...].reshape(1, 128)
    occ_first = jnp.sum(jnp.where(pair[:, 0:1] == table, occ, 0.0), axis=1, keepdims=True)
    occ_second = jnp.sum(jnp.where(pair[:, 1:2] == table, occ, 0.0), axis=1, keepdims=True)
    vir = vir_ref[...].reshape(1, NV)
    blocks = lax.broadcasted_iota(jnp.int32, (1, 8), 1)
    a_pick = jnp.sum(
        jnp.where(blocks == r // 2, aorb_ref[...].astype(F32).reshape(1, 8), 0.0),
        axis=1,
        keepdims=True,
    )
    orbitals = lax.broadcasted_iota(jnp.int32, (1, NV), 1).astype(F32)
    vir_a = jnp.sum(jnp.where(orbitals == a_pick, vir, 0.0), axis=1, keepdims=True)
    vir_b = jnp.where(r % 2 == 0, vir[:, 0:AB], vir[:, AB:NV])
    denom = (occ_first + occ_second) - (vir_a + vir_b)

    wait_for(near_in.at[pl.ds(0, PLANE - 1)], near_send)
    wait_for(far_in.at[pl.ds(0, PLANE - 1)], far_send)
    wait_for(units.at[0, pl.ds(0, 7)], up_send)
    for i in range(STAGES):
        drain(i)
    for i in (2, 3):
        sum_z(i)
        give(i)
    others = other_ref[...]
    for q in range(STAGES - 1):
        source = (zl + 1 + q) % STAGES
        wait_for(from_z.at[source], z_recv.at[source])
        others = others + from_z[source, :, 0:AB]
    out_ref[...] = old_ref[...] + (to_z[zl, :, 0:AB] + others) / denom
    for i in range(STAGES):

        @pl.when(zl != i)
        def _(i=i):
            z_copy(i).wait_send()


def local(
    integrals, amplitudes, old_amps, other_terms, occ_energy, vir_energy, pair_occ, a_orbitals
):
    vmem = pl.BlockSpec(memory_space=pltpu.VMEM)
    dma = pltpu.SemaphoreType.DMA
    return pl.pallas_call(
        kernel,
        out_shape=jax.ShapeDtypeStruct((8, AB), F32),
        in_specs=[pl.BlockSpec(memory_space=pltpu.HBM)] * 8,
        out_specs=vmem,
        scratch_shapes=[
            pltpu.VMEM((AB, NV), F32),
            pltpu.VMEM((8 * 64, DEPTH), F32),
            pltpu.VMEM((8, AB), F32),
            pltpu.VMEM((8, AB), F32),
            pltpu.VMEM((128,), F32),
            pltpu.VMEM((NV,), F32),
            pltpu.VMEM((2, 8), jnp.int32),
            pltpu.VMEM((8,), jnp.int32),
            pltpu.VMEM((PLANE, 8, 128), F32),
            pltpu.VMEM((PLANE, 8, 128), F32),
            pltpu.VMEM((PLANE, 8, 256), F32),
            pltpu.VMEM((PLANE, 8, 256), F32),
            pltpu.VMEM((STAGES - 1, UNIT, 128), F32),
            pltpu.VMEM((STAGES, ROWS, UNIT, 128), F32),
            pltpu.VMEM((ABP, NVP), BF16),
            pltpu.VMEM((ABP, NVP), BF16),
            pltpu.VMEM((2, WINDOW, 128), F32),
            pltpu.VMEM((256, 128), F32),
            pltpu.VMEM((STAGES, ABP, 128), F32),
            pltpu.VMEM((STAGES, 2, 8, 8, ABP), F32),
            pltpu.VMEM((STAGES, 8, 8, ABP), F32),
            pltpu.VMEM((STAGES, 3, 8, ABP), F32),
            pltpu.VMEM((STAGES, 4, 8, ABP), F32),
            pltpu.VMEM((STAGES, 8, ABP), F32),
            pltpu.VMEM((STAGES, 8, ABP), F32),
            pltpu.SemaphoreType.REGULAR,
            pltpu.SemaphoreType.REGULAR,
            dma((8,)),
            dma,
            dma,
            dma,
            dma,
            dma,
            dma((STAGES,)),
            dma((STAGES,)),
            dma((STAGES, 15)),
            dma((STAGES,)),
            dma((STAGES,)),
            dma((STAGES,)),
            dma((STAGES,)),
            dma((STAGES,)),
            dma((STAGES,)),
            dma((STAGES,)),
        ],
        compiler_params=pltpu.CompilerParams(
            collective_id=0, has_side_effects=True, vmem_limit_bytes=60 * 1024 * 1024
        ),
        cost_estimate=pl.CostEstimate(
            flops=6 * 512 * AB * NV, bytes_accessed=4 * AB * NV, transcendentals=0
        ),
    )(
        integrals,
        amplitudes.reshape(8 * 64, DEPTH),
        old_amps,
        other_terms,
        occ_energy,
        vir_energy,
        pair_occ.T,
        a_orbitals,
    )


def solution(mesh):
    in_specs = (
        P("row", "col"),
        P("col", None, "row"),
        P("col", "row"),
        P("col", "row"),
        P(),
        P(),
        P("col", None),
        P(),
    )
    out_specs = P("col", "row")
    return jax.shard_map(local, mesh=mesh, in_specs=in_specs, out_specs=out_specs, check_vma=False)
```

```python
import jax
import jax.numpy as jnp
from jax import lax
from jax.experimental import pallas as pl
from jax.experimental.pallas import tpu as pltpu
from jax.sharding import PartitionSpec as P

NV = 1200
MESH = pl.DeviceIdType.MESH
X = 8
PLANE = 16
STAGES = 4
ROWS = 16
OTHER_TURN = 2
DEPTH = 75
UNIT = 80
AB = 600
ABP = 640
NVP = 1280
WINDOW = 768
SHIFT = 88
F32 = jnp.float32
BF16 = jnp.bfloat16

OWN_LONG, OWN_SHORT, OTHER_LONG, OTHER_SHORT = 0, 4, 7, 11


def far_first(n, count):
    return count // 2 + (n + 1) // 2 * (1 - 2 * (n % 2))


def kernel(
    integrals_hbm,
    amps_hbm,
    old_hbm,
    other_hbm,
    occ_hbm,
    vir_hbm,
    pair_hbm,
    aorb_hbm,
    out_ref,
    integ,
    amps_ref,
    old_ref,
    other_ref,
    occ_ref,
    vir_ref,
    pair_ref,
    aorb_ref,
    near_out,
    near_in,
    far_out,
    far_in,
    units_out,
    units,
    high,
    low,
    panel,
    last_panel,
    total,
    partial,
    from_core,
    join,
    from_y,
    to_z,
    from_z,
    half_here,
    facing_here,
    load_sem,
    near_send,
    near_recv,
    far_send,
    far_recv,
    up_send,
    up_recv,
    unit_send,
    unit_recv,
    core_send,
    core_recv,
    join_recv,
    y_send,
    y_recv,
    z_send,
    z_recv,
):
    r = lax.axis_index("row")
    k = lax.axis_index("col")
    x, zh = r % X, r // X
    zl, m = k // PLANE, k % PLANE
    y, core = m // 2, m % 2
    right = zh * X + (x + 1) % X
    left = zh * X + (x + X - 1) % X
    facing = (r + X) % ROWS

    loads = [
        pltpu.make_async_copy(source, target, load_sem.at[n])
        for n, (source, target) in enumerate(
            (
                (amps_hbm, amps_ref),
                (integrals_hbm, integ),
                (old_hbm, old_ref),
                (other_hbm, other_ref),
                (occ_hbm, occ_ref),
                (vir_hbm, vir_ref),
                (pair_hbm, pair_ref),
                (aorb_hbm, aorb_ref),
            )
        )
    ]
    loads[0].start()

    barrier = pltpu.get_barrier_semaphore()

    def greet(row, col):
        pl.semaphore_signal(barrier, inc=1, device_id=(row, col), device_id_type=MESH)

    def greet_plane(j, carry):
        greet(r, zl * PLANE + (m + j) % PLANE)
        return carry

    lax.fori_loop(1, PLANE, greet_plane, 0)
    greet(right, k)
    greet(left, k)

    for j in range(1, STAGES):

        @pl.when(zl + j < STAGES)
        def _(j=j):
            greet(r, k + j * PLANE)

    @pl.when(zh == 0)
    def _():
        for j in range(STAGES):
            greet(facing, j * PLANE + m)

    def tile_of(plane, t):
        return amps_ref[pl.ds(plane % STAGES * PLANE + t, 8, stride=64), :]

    near_out[...] = jnp.zeros_like(near_out)
    far_out[...] = jnp.zeros_like(far_out)
    loads[0].wait()
    for load in loads[1:]:
        load.start()
    for t in range(PLANE):
        near_out[t, :, 0:DEPTH] = tile_of(zl, t)
    pl.semaphore_wait(barrier, PLANE - 1 + 2 + zl + STAGES * zh)

    def answer(sem, row, col):
        pl.semaphore_signal(sem, inc=1, device_id=(row, col), device_id_type=MESH)

    for j in range(1, STAGES):

        @pl.when(zl >= j)
        def _(j=j):
            answer(half_here, r, k - j * PLANE)

    @pl.when(zh == 1)
    def _():
        for j in range(STAGES):
            answer(facing_here, facing, j * PLANE + m)

    def send_tiles(source, target, send_sem, recv_sem):
        def one(n, carry):
            t = (m + far_first(n, PLANE)) % PLANE
            pltpu.make_async_remote_copy(
                src_ref=source.at[t],
                dst_ref=target.at[m],
                send_sem=send_sem,
                recv_sem=recv_sem,
                device_id=(r, zl * PLANE + t),
                device_id_type=MESH,
            ).start()
            return carry

        lax.fori_loop(0, PLANE - 1, one, 0)
        target[m] = source[m]

    def wait_for(some, sem):
        pltpu.make_async_copy(some, some, sem).wait()

    send_tiles(near_out, near_in, near_send, near_recv)
    for t in range(PLANE):
        for q in range(STAGES - 1):
            far_out[t, :, q * DEPTH : (q + 1) * DEPTH] = tile_of(zl + 1 + q, t)
    send_tiles(far_out, far_in, far_send, far_recv)

    def split(v):
        hi = v.astype(BF16)
        return hi, (v - hi.astype(F32)).astype(BF16)

    def split_integrals():
        loads[1].wait()
        last = NV // 128 * 128
        for part in (high, low):
            part[:, last:] = jnp.zeros((ABP, NVP - last), BF16)

        def chunk(n, carry):
            rows = pl.ds(pl.multiple_of(n * 128, 128), 128)
            hi, lo = split(integ[rows, :])
            high[rows, 0:NV] = hi
            low[rows, 0:NV] = lo
            return carry

        lax.fori_loop(0, 4, chunk, 0)
        pad = jnp.zeros((ABP - AB, NV), BF16)
        hi, lo = split(integ[512:AB, :])
        high[512:ABP, 0:NV] = jnp.concatenate([hi, pad], axis=0)
        low[512:ABP, 0:NV] = jnp.concatenate([lo, pad], axis=0)

    def way(i, lane):
        sign = 1 if lane in (OWN_LONG, OTHER_SHORT) else -1
        return sign * (1 - 2 * (i % 2))

    def copy_unit(i, lane, h, origin):
        return pltpu.make_async_remote_copy(
            src_ref=units.at[i, origin],
            dst_ref=units.at[i, origin],
            send_sem=unit_send.at[i],
            recv_sem=unit_recv.at[i, lane + h],
            device_id=(zh * X + (x + X + way(i, lane)) % X, k),
            device_id_type=MESH,
        )

    def origin_of(i, lane, h):
        plane = zh if lane in (OWN_LONG, OWN_SHORT) else 1 - zh
        return plane * X + (x + X - h * way(i, lane)) % X

    def hop(i, lane, h):
        return copy_unit(i, lane, h, origin_of(i, lane, h - 1))

    def land(i, lane, h):
        copy_unit(i, lane, h, origin_of(i, lane, h)).wait_recv()

    def multiply(i, start, width, units_here):
        columns = pl.ds(pl.multiple_of(start, 128), width)
        hi, lo = split(units_here)
        both = jnp.dot(
            high[:, columns], jnp.concatenate([hi, lo], axis=1), preferred_element_type=F32
        )
        rest = jnp.dot(low[:, columns], hi, preferred_element_type=F32)
        total[i] += both[:, 0:128] + (both[:, 128:256] + rest)

    def place(i, plane, u):
        panel[plane, pl.ds(plane * SHIFT + u * DEPTH, DEPTH), :] = units[i, plane * X + u, 0:DEPTH]

    def add(i, plane):
        for u in range(X):
            place(i, plane, u)
        multiply(i, plane * 512, WINDOW, panel[plane])

    other, farthest = 1 - zh, (x + X // 2) % X
    last_row = other * SHIFT + farthest * DEPTH

    def add_first(i):
        for n in range(1, X):
            place(i, other, (farthest + n) % X)
        panel[other, pl.ds(last_row, DEPTH), :] = jnp.zeros((DEPTH, 128), F32)
        multiply(i, other * 512, WINDOW, panel[other])

    def add_last(i):
        last_panel[pl.ds(last_row % 128, DEPTH), :] = units[i, other * X + farthest, 0:DEPTH]
        multiply(i, other * 512 + last_row // 128 * 128, 256, last_panel[...])

    def unit_to(source, plane, row, recv_sem):
        return pltpu.make_async_remote_copy(
            src_ref=source,
            dst_ref=units.at[zl, r],
            send_sem=up_send,
            recv_sem=recv_sem,
            device_id=(row, plane * PLANE + m),
            device_id_type=MESH,
        )

    def to_half():
        for q in range(STAGES - 1):
            unit_to(units_out.at[q], (zl + 1 + q) % STAGES, r, up_recv.at[zl]).start()

    def to_facing():
        arrived = unit_recv.at[zl, 0]
        unit_to(units.at[zl, r], zl, facing, arrived).start()
        for q in range(STAGES - 1):
            unit_to(units_out.at[q], (zl + 1 + q) % STAGES, facing, arrived).start()

    def begin(i):
        @pl.when(zl != i)
        def _():
            wait_for(units.at[i, r], up_recv.at[i])

        step(i, 0, True)

    def make_units():
        wait_for(near_in.at[pl.ds(0, PLANE - 1)], near_recv)
        units[zl, r] = jnp.transpose(near_in[...].reshape(128, 128))[0:UNIT]
        wait_for(far_in.at[pl.ds(0, PLANE - 1)], far_recv)
        turned = jnp.transpose(far_in[...].reshape(128, 256))
        for q in range(STAGES - 1):
            units_out[q] = turned[q * DEPTH : q * DEPTH + UNIT]

    def step(i, s, own):
        long, short = (OWN_LONG, OWN_SHORT) if own else (OTHER_LONG, OTHER_SHORT)
        if s == 0 and not own:
            wait_for(units.at[i, facing], unit_recv.at[i, 0])
        for lane, hops in ((long, 4), (short, 3)):
            if 1 <= s <= hops:
                land(i, lane, s)
            if s < hops:
                hop(i, lane, s + 1).start()

    def core_copy(i):
        return pltpu.make_async_remote_copy(
            src_ref=partial.at[i, 1 - core],
            dst_ref=from_core.at[i],
            send_sem=core_send.at[i],
            recv_sem=core_recv.at[i],
            device_id=(r, zl * PLANE + y * 2 + 1 - core),
            device_id_type=MESH,
        )

    def sum_cores(i):
        ladder = jnp.transpose(total[i])
        for t in range(PLANE):
            partial[i, t % 2, t // 2] = ladder[8 * t : 8 * t + 8]
        core_copy(i).start()

    def y_copy(i, block, away, target, recv_sem):
        return pltpu.make_async_remote_copy(
            src_ref=partial.at[i, core, (y + 8 + block) % 8],
            dst_ref=target,
            send_sem=y_send.at[i],
            recv_sem=recv_sem,
            device_id=(r, zl * PLANE + (y + 8 + away) % 8 * 2 + core),
            device_id_type=MESH,
        )

    def sum_y(i):
        core_copy(i).wait_recv()
        partial[i, core] = partial[i, core] + from_core[i]
        y_copy(i, 4, 2 - 4 * (i % 2), join.at[i, 2], join_recv.at[i]).start()
        for n, side in enumerate((1, -1)):
            y_copy(i, 3 * side, side, join.at[i, n], join_recv.at[i]).start()
        for n, side in enumerate((1, -1)):
            y_copy(i, side, side, from_y.at[i, n], y_recv.at[i]).start()

    def join_y(i):
        wait_for(join.at[i], join_recv.at[i])
        for n, away in enumerate((2, -2, 2 - 4 * (i % 2))):
            block = (y + 8 + away) % 8
            partial[i, core, block] = partial[i, core, block] + join[i, n]
        for n, side in enumerate((2, -2)):
            y_copy(i, side, side, from_y.at[i, 2 + n], y_recv.at[i]).start()

    def z_copy(i):
        return pltpu.make_async_remote_copy(
            src_ref=to_z.at[i],
            dst_ref=from_z.at[zl],
            send_sem=z_send.at[i],
            recv_sem=z_recv.at[zl],
            device_id=(r, i * PLANE + m),
            device_id_type=MESH,
        )

    def sum_z(i):
        wait_for(from_y.at[i], y_recv.at[i])
        value = partial[i, core, y]
        for j in range(4):
            value = value + from_y[i, j]
        to_z[i] = value

    def give(i):
        @pl.when(zl != i)
        def _():
            z_copy(i).start()

    def drain(i):
        wait_for(units.at[i, pl.ds(0, 14)], unit_send.at[i])
        core_copy(i).wait_send()
        wait_for(partial.at[i, 0, pl.ds(0, 7)], y_send.at[i])

    def pair_step(n, first, s, own):
        @pl.when((n - first - s >= 0) & (n - first - s < 2))
        def _():
            for b in range(2):
                step((n - first - s) * 2 + b, s, own)

    total[...] = jnp.zeros_like(total)
    panel[...] = jnp.zeros_like(panel)
    last_panel[...] = jnp.zeros_like(last_panel)
    split_integrals()
    make_units()

    @pl.when(zh == 1)
    def _():
        to_facing()

    @pl.when(zl < STAGES - 1)
    def _():
        pl.semaphore_wait(half_here, STAGES - 1 - zl)

    to_half()

    for i in range(STAGES):
        begin(i)

    def turn(n, carry):
        for s in (4, 3, 2, 1):

            @pl.when(n == s)
            def _(s=s):
                for i in range(STAGES):
                    step(i, s, True)

        for s in (4, 3, 2, 1, 0):
            pair_step(n, OTHER_TURN, s, False)

        @pl.when((n == 1) & (zh == 0))
        def _():
            pl.semaphore_wait(facing_here, STAGES)
            to_facing()

        @pl.when((n == OTHER_TURN + 2) | (n == OTHER_TURN + 3))
        def _():
            for b in range(2):
                add((n - OTHER_TURN - 2) * 2 + b, zh)

        @pl.when(n == OTHER_TURN + 3)
        def _():
            add_first(0)
            add_first(1)

        return carry

    lax.fori_loop(1, OTHER_TURN + 4, turn, 0)
    for i in range(STAGES):
        step(i, 4 - i // 2, False)
    for i in (0, 1):
        add_last(i)
        sum_cores(i)
    for i in (2, 3):
        add_first(i)
    for i in (0, 1):
        sum_y(i)
    for i in (2, 3):
        step(i, 4, False)
        add_last(i)
        sum_cores(i)
    for i in (0, 1):
        join_y(i)
    for i in (2, 3):
        sum_y(i)
    for i in (0, 1):
        sum_z(i)
        give(i)
    for i in (2, 3):
        join_y(i)

    for load in loads[2:]:
        load.wait()
    pair = jnp.transpose(
        jnp.concatenate(
            [
                jnp.concatenate([pair_ref[...].astype(F32), jnp.zeros((2, 120), F32)], axis=1),
                jnp.zeros((126, 128), F32),
            ],
            axis=0,
        )
    )[0:8]
    table = lax.broadcasted_iota(jnp.int32, (8, 128), 1).astype(F32)
    occ = occ_ref[...].reshape(1, 128)
    occ_first = jnp.sum(jnp.where(pair[:, 0:1] == table, occ, 0.0), axis=1, keepdims=True)
    occ_second = jnp.sum(jnp.where(pair[:, 1:2] == table, occ, 0.0), axis=1, keepdims=True)
    vir = vir_ref[...].reshape(1, NV)
    blocks = lax.broadcasted_iota(jnp.int32, (1, 8), 1)
    a_pick = jnp.sum(
        jnp.where(blocks == r // 2, aorb_ref[...].astype(F32).reshape(1, 8), 0.0),
        axis=1,
        keepdims=True,
    )
    orbitals = lax.broadcasted_iota(jnp.int32, (1, NV), 1).astype(F32)
    vir_a = jnp.sum(jnp.where(orbitals == a_pick, vir, 0.0), axis=1, keepdims=True)
    vir_b = jnp.where(r % 2 == 0, vir[:, 0:AB], vir[:, AB:NV])
    denom = (occ_first + occ_second) - (vir_a + vir_b)

    wait_for(near_in.at[pl.ds(0, PLANE - 1)], near_send)
    wait_for(far_in.at[pl.ds(0, PLANE - 1)], far_send)
    wait_for(units.at[0, pl.ds(0, 7)], up_send)
    for i in range(STAGES):
        drain(i)
    for i in (2, 3):
        sum_z(i)
        give(i)
    others = other_ref[...]
    for q in range(STAGES - 1):
        source = (zl + 1 + q) % STAGES
        wait_for(from_z.at[source], z_recv.at[source])
        others = others + from_z[source, :, 0:AB]
    out_ref[...] = old_ref[...] + (to_z[zl, :, 0:AB] + others) / denom
    for i in range(STAGES):

        @pl.when(zl != i)
        def _(i=i):
            z_copy(i).wait_send()


def local(
    integrals, amplitudes, old_amps, other_terms, occ_energy, vir_energy, pair_occ, a_orbitals
):
    vmem = pl.BlockSpec(memory_space=pltpu.VMEM)
    dma = pltpu.SemaphoreType.DMA
    return pl.pallas_call(
        kernel,
        out_shape=jax.ShapeDtypeStruct((8, AB), F32),
        in_specs=[pl.BlockSpec(memory_space=pltpu.HBM)] * 8,
        out_specs=vmem,
        scratch_shapes=[
            pltpu.VMEM((AB, NV), F32),
            pltpu.VMEM((8 * 64, DEPTH), F32),
            pltpu.VMEM((8, AB), F32),
            pltpu.VMEM((8, AB), F32),
            pltpu.VMEM((128,), F32),
            pltpu.VMEM((NV,), F32),
            pltpu.VMEM((2, 8), jnp.int32),
            pltpu.VMEM((8,), jnp.int32),
            pltpu.VMEM((PLANE, 8, 128), F32),
            pltpu.VMEM((PLANE, 8, 128), F32),
            pltpu.VMEM((PLANE, 8, 256), F32),
            pltpu.VMEM((PLANE, 8, 256), F32),
            pltpu.VMEM((STAGES - 1, UNIT, 128), F32),
            pltpu.VMEM((STAGES, ROWS, UNIT, 128), F32),
            pltpu.VMEM((ABP, NVP), BF16),
            pltpu.VMEM((ABP, NVP), BF16),
            pltpu.VMEM((2, WINDOW, 128), F32),
            pltpu.VMEM((256, 128), F32),
            pltpu.VMEM((STAGES, ABP, 128), F32),
            pltpu.VMEM((STAGES, 2, 8, 8, ABP), F32),
            pltpu.VMEM((STAGES, 8, 8, ABP), F32),
            pltpu.VMEM((STAGES, 3, 8, ABP), F32),
            pltpu.VMEM((STAGES, 4, 8, ABP), F32),
            pltpu.VMEM((STAGES, 8, ABP), F32),
            pltpu.VMEM((STAGES, 8, ABP), F32),
            pltpu.SemaphoreType.REGULAR,
            pltpu.SemaphoreType.REGULAR,
            dma((8,)),
            dma,
            dma,
            dma,
            dma,
            dma,
            dma((STAGES,)),
            dma((STAGES,)),
            dma((STAGES, 15)),
            dma((STAGES,)),
            dma((STAGES,)),
            dma((STAGES,)),
            dma((STAGES,)),
            dma((STAGES,)),
            dma((STAGES,)),
            dma((STAGES,)),
        ],
        compiler_params=pltpu.CompilerParams(
            collective_id=0, has_side_effects=True, vmem_limit_bytes=60 * 1024 * 1024
        ),
        cost_estimate=pl.CostEstimate(
            flops=6 * 512 * AB * NV, bytes_accessed=4 * AB * NV, transcendentals=0
        ),
    )(
        integrals,
        amplitudes.reshape(8 * 64, DEPTH),
        old_amps,
        other_terms,
        occ_energy,
        vir_energy,
        pair_occ.T,
        a_orbitals,
    )


def solution(mesh):
    in_specs = (
        P("row", "col"),
        P("col", None, "row"),
        P("col", "row"),
        P("col", "row"),
        P(),
        P(),
        P("col", None),
        P(),
    )
    out_specs = P("col", "row")
    return jax.shard_map(local, mesh=mesh, in_specs=in_specs, out_specs=out_specs, check_vma=False)
```
